32 devices in a mesh: gz: 4 (over x, core), ma: 8 (over z, y).
Axes of the slice: x: 2, y: 2, z: 4, core: 2. Of those that a mesh axis runs over, the one named last changes fastest.
Arguments:
- forward: float32 [4, 2, 1024, 4096], P('gz', None, 'ma'), may hold values from -6 to 6
- cotangent: float32 [4, 2, 1024, 4096], P('gz', None, 'ma'), may hold values from -6 to 6
- mode_order: int32 [1024], replicated, may hold values from 0 to 1023, each once
- region: int32 [128, 128], replicated, may hold values from 0 to 7
- chi: float32 [8], replicated, may hold values from 0.5 to 2
- phase: float32 [1024, 4096], P('ma'), may hold values from -3.140625 to 3.140625
- loss: float32 [4, 1024], P('gz', 'ma'), may hold values from 0.5 to 1
Outputs:
- adjoint: float32 [4, 2, 1024, 4096], P('gz', None, 'ma')
The draws below stay inside these ranges and needn't reach their ends.
Inputs may be any that keep to these rules, and one draw needn't show every extreme that they name: Each number appears once; stored mode m has order mode_order[m] // 32 along the first transverse coordinate and mode_order[m] % 32 along the second.
All inputs are finite; a program needn't handle non-finite values.
Results may differ from the reference program's by a relative error of at most 0.0003.
Values sent between devices are 32-bit elements; how exact they have to be, the bound alone decides.
A program may use at most 320 MiB of HBM per device.

```python
import math
import jax
import jax.numpy as jnp
from jax import lax

HG_ORDER = 32
MODES = 1024
TIME = 4096
GRID = 128
REGIONS = 8
ZL = 4
N_MA = 8


def with_ends(array, stream_key, smallest, top_value):
    longest = array.shape.index(max(array.shape))
    spots = []
    for shift in (0, 1):
        where = [jax.random.randint(jax.random.fold_in(stream_key, axis), (), 0, length) for axis, length in enumerate(array.shape)]
        where[longest] = (where[longest] + shift) % array.shape[longest]
        spots.append(tuple(where))
    return array.at[spots[0]].set(smallest).at[spots[1]].set(top_value)


def block_scale(key, dims, split, smallest, largest):
    factor_of, own = 1.0, jax.random.fold_in(key, 6)
    for axis_at, shards_of in split:
        heights = jnp.exp(jax.random.uniform(jax.random.fold_in(own, axis_at), (shards_of,), jnp.float32, smallest / len(split), largest / len(split)))
        factor_of = factor_of * jnp.repeat(heights, dims[axis_at] // shards_of).reshape([-1 if axis == axis_at else 1 for axis in range(len(dims))])
    return factor_of


def scatter_about(rng, shape, width, bound, split=(), kind=jnp.bfloat16):
    entries = width * jax.random.normal(rng, shape, jnp.float32)
    if split:
        entries = entries * block_scale(rng, shape, split, -0.22, 0.18)
    return jnp.clip(entries, -bound, bound).astype(kind)


def setup_inputs(seed: int = 0) -> dict:
    splits = jax.random.split(jax.random.key(seed), 8)
    return {
        "forward": scatter_about(splits[0], (ZL, 2, MODES, TIME), 1.0, 6.0, ((0, 4), (2, 8)), jnp.float32),
        "cotangent": scatter_about(splits[1], (ZL, 2, MODES, TIME), 1.0, 6.0, ((0, 4), (2, 8)), jnp.float32),
        "mode_order": jax.random.permutation(splits[2], MODES).astype(jnp.int32),
        "region": with_ends(jax.random.randint(splits[3], (GRID, GRID), 0, REGIONS), jax.random.fold_in(splits[3], 1), 0, REGIONS - 1).astype(jnp.int32),
        "chi": jnp.clip(jnp.exp(jax.random.uniform(splits[4], (REGIONS,), jnp.float32, math.log(0.5), math.log(2.0))), 0.5, 2.0),
        "phase": jnp.clip(jax.random.uniform(splits[5], (MODES, TIME), jnp.float32, -3.140625, 3.140625), -3.140625, 3.140625),
        "loss": jnp.clip(0.5 + 0.5 * jax.random.uniform(splits[6], (ZL, MODES), jnp.float32) ** block_scale(splits[6], (ZL, MODES), ((0, 4), (1, 8)), -0.2, 0.2), 0.5, 1.0),
    }


gamma_kerr = 2.0
half_width = 10.0

def hermite_table(grid_points, degrees):
    spacing = 2.0 * half_width / grid_points
    coords = (jnp.arange(grid_points, dtype=jnp.float32) - (grid_points - 1) / 2.0) * spacing
    columns = [jnp.exp(-0.5 * coords * coords) * math.pi ** (-0.25)]
    if degrees > 1:
        columns.append(math.sqrt(2.0) * coords * columns[0])
    for degree in range(2, degrees):
        following = math.sqrt(2.0 / degree) * coords * columns[degree - 1] - math.sqrt((degree - 1.0) / degree) * columns[degree - 2]
        columns.append(following)
    return jnp.stack(columns, axis=1) * math.sqrt(spacing)

def modes_to_grid(fields, table):
    partial_grid = jnp.einsum('...pqt,yq->...pyt', fields, table, precision=lax.Precision.HIGHEST)
    return jnp.einsum('...pyt,xp->...xyt', partial_grid, table, precision=lax.Precision.HIGHEST)

def grid_to_modes(values, table):
    partial_grid = jnp.einsum('...xyt,xp->...pyt', values, table, precision=lax.Precision.HIGHEST)
    return jnp.einsum('...pyt,yq->...pqt', partial_grid, table, precision=lax.Precision.HIGHEST)

def kerr_adjoint(forward, cotangent, table, chi_grid, inverse, mode_order):
    leading = forward.shape[:-2]
    samples = forward.shape[-1]
    degrees = table.shape[1]

    def ordered_grid(fields):
        ordered = jnp.take(fields, inverse, axis=-2)
        return ordered.reshape(leading + (degrees, degrees, samples))
    field_grid = modes_to_grid(ordered_grid(forward), table)
    cot_grid = modes_to_grid(ordered_grid(cotangent), table)
    field_real = field_grid[..., 0, :, :, :]
    field_imag = field_grid[..., 1, :, :, :]
    cot_real = cot_grid[..., 0, :, :, :]
    cot_imag = cot_grid[..., 1, :, :, :]
    strength = gamma_kerr * chi_grid[:, :, None]
    intensity = field_real * field_real + field_imag * field_imag
    cross = 2.0 * field_real * field_imag
    grad_real = strength * (-cross * cot_real + (intensity + 2.0 * field_real * field_real) * cot_imag)
    grad_imag = strength * (-(intensity + 2.0 * field_imag * field_imag) * cot_real + cross * cot_imag)
    projected = grid_to_modes(jnp.stack([grad_real, grad_imag], axis=-4), table)
    flat = projected.reshape(leading + (degrees * degrees, samples))
    return jnp.take(flat, mode_order, axis=-2)

def reference(forward, cotangent, mode_order, region, chi, phase, loss):
    table = hermite_table(GRID, HG_ORDER)
    matches = (region[:, :, None] == jnp.arange(REGIONS, dtype=jnp.int32)[None, None, :]).astype(jnp.float32)
    chi_grid = lax.optimization_barrier(jnp.sum(matches * chi[None, None, :], axis=-1))
    inverse = jnp.zeros((MODES,), jnp.int32).at[mode_order].set(jnp.arange(MODES, dtype=jnp.int32))
    block_size = TIME // N_MA

    def one_block(block_index):
        start = (block_index * block_size).astype(jnp.int32)
        forward_block = lax.dynamic_slice_in_dim(forward, start, block_size, 3)
        cot_block = lax.dynamic_slice_in_dim(cotangent, start, block_size, 3)
        return kerr_adjoint(forward_block, cot_block, table, chi_grid, inverse, mode_order)
    pieces = lax.map(one_block, jnp.arange(N_MA, dtype=jnp.int32))
    kerr = jnp.moveaxis(pieces, 0, 3).reshape(ZL, 2, MODES, TIME)
    source = cotangent + kerr
    wave = lax.complex(source[:, 0], source[:, 1])
    spectrum = jnp.fft.fft(wave, axis=-1) * lax.complex(jnp.cos(phase), -jnp.sin(phase))[None]
    back = jnp.fft.ifft(spectrum, axis=-1)
    dispersed = jnp.stack([jnp.real(back), jnp.imag(back)], axis=1)

    def backward_step(carry, inputs):
        term, factor = inputs
        value = term + factor[None, :, None] * carry
        return (value, value)
    start_carry = jnp.zeros_like(dispersed[0])
    final_carry, adjoint = lax.scan(backward_step, start_carry, (dispersed, loss), reverse=True)
    return adjoint
```

```python
import functools
import math

import jax
import jax.numpy as jnp
import ml_dtypes
import numpy as np
from jax import lax
from jax.experimental import pallas as pl
from jax.experimental.pallas import tpu as pltpu
from jax.sharding import PartitionSpec as P

HG_ORDER = 32
GRID = 128
REGIONS = 8
LANES = 128
GROUP = 8

gamma_kerr = 2.0
half_width = 10.0

f32 = jnp.float32
bf16 = jnp.bfloat16


def hermite_table(grid_points, degrees):
    spacing = 2.0 * half_width / grid_points
    coords = (np.arange(grid_points, dtype=np.float64) - (grid_points - 1) / 2.0) * spacing
    columns = [np.exp(-0.5 * coords * coords) * math.pi ** (-0.25)]
    columns.append(math.sqrt(2.0) * coords * columns[0])
    for degree in range(2, degrees):
        columns.append(
            math.sqrt(2.0 / degree) * coords * columns[degree - 1]
            - math.sqrt((degree - 1.0) / degree) * columns[degree - 2]
        )
    return (np.stack(columns, axis=1) * math.sqrt(spacing)).astype(np.float32)


def host_parts(array):
    array = np.asarray(array, np.float32)
    high = array.astype(ml_dtypes.bfloat16)
    low = (array - high.astype(np.float32)).astype(ml_dtypes.bfloat16)
    return high, low


def parts(value):
    high = value.astype(bf16)
    low = (value - high.astype(f32)).astype(bf16)
    return high, low


def mm(left, right):
    return jnp.dot(left, right, preferred_element_type=f32)


def kerr_constants():
    table = hermite_table(GRID, HG_ORDER)
    eye = np.eye(GROUP, dtype=np.float32)
    spread = np.einsum("yq,ab->yabq", table, eye).reshape(GRID * GROUP, GROUP * HG_ORDER)
    gather = np.einsum("yq,ab->aqyb", table, eye).reshape(GROUP * HG_ORDER, GRID * GROUP)
    spread_high, spread_low = host_parts(spread)
    gather_high, gather_low = host_parts(gather)
    table_high, table_low = host_parts(table)
    return (
        np.concatenate([spread_high, spread_high, spread_low], axis=1),
        np.concatenate([table_high, table_high, table_low], axis=1),
        np.concatenate([gather_high, gather_high, gather_low], axis=1),
        np.ascontiguousarray(table.T),
    )


def kerr_kernel(
    x_ref, perm_ref, back_ref, spread_ref, table_ref, gather_ref, flip_ref, chi_ref, out_ref,
    xh, xl, p3, g1, r3, qh, ql,
):
    shards, _, local, _ = x_ref.shape
    groups = HG_ORDER // GROUP
    span = GROUP * HG_ORDER

    @pl.loop(0, shards)
    def _(s):
        value = jnp.concatenate([x_ref[s, c] for c in range(4)], axis=1)
        high, low = parts(value)
        rows = pl.ds(pl.multiple_of(s * local, local), local)
        xh[rows, :] = high
        xl[rows, :] = low

    @pl.loop(0, groups)
    def _(g):
        rows = pl.ds(pl.multiple_of(g * span, span), span)
        high = mm(perm_ref[rows, :], xh[...]).astype(bf16)
        p3[g, 0:span, :] = high
        p3[g, 2 * span : 3 * span, :] = high
        p3[g, span : 2 * span, :] = mm(perm_ref[rows, :], xl[...]).astype(bf16)

    points = 16
    for pair in range(groups // 2):

        @pl.loop(0, GRID // points)
        def _(b):
            rows = pl.ds(pl.multiple_of(b * points * GROUP, points * GROUP), points * GROUP)
            ys = pl.ds(b * points, points)
            both = [
                mm(spread_ref[rows, :], p3[2 * pair + i]).reshape(points, GROUP, 4 * LANES)
                for i in range(2)
            ]
            high, low = parts(jnp.concatenate(both, axis=1))
            g1[ys, pair * 16 : pair * 16 + 16, :] = high
            g1[ys, HG_ORDER + pair * 16 : HG_ORDER + pair * 16 + 16, :] = low

    def line(y):
        stored = g1[y]
        grid = mm(table_ref[...], jnp.concatenate([stored, stored[:HG_ORDER]], axis=0))
        er, ei, cr, ci = (grid[:, i * LANES : (i + 1) * LANES] for i in range(4))
        rr, ii = er * er, ei * ei
        intensity = rr + ii
        cross = 2.0 * er * ei
        real = (intensity + 2.0 * rr) * ci - cross * cr
        imag = cross * ci - (intensity + 2.0 * ii) * cr
        high, low = parts(jnp.concatenate([real, imag], axis=1))
        weight_high, weight_low = parts(flip_ref[...] * chi_ref[pl.ds(y, 1), :])
        weights = jnp.concatenate([weight_high, weight_high, weight_low], axis=1)
        return mm(weights, jnp.concatenate([high, low, high], axis=0))

    total = GRID * GROUP
    step_lines = 4

    @pl.loop(0, GRID // step_lines)
    def _(b):
        got = [line(b * step_lines + i) for i in range(step_lines)]
        rows = step_lines * GROUP
        at = pl.multiple_of(b * rows, rows)
        for g in range(groups):
            high, low = parts(
                jnp.concatenate([v[g * GROUP : (g + 1) * GROUP] for v in got], axis=0)
            )
            r3[g, pl.ds(at, rows), :] = high
            r3[g, pl.ds(total + at, rows), :] = low
            r3[g, pl.ds(2 * total + at, rows), :] = high

    @pl.loop(0, groups)
    def _(g):
        high, low = parts(mm(gather_ref[...], r3[g]))
        rows = pl.ds(pl.multiple_of(g * span, span), span)
        qh[rows, :] = high
        ql[rows, :] = low

    @pl.loop(0, shards)
    def _(s):
        rows = pl.ds(pl.multiple_of(s * local, local), local)
        value = mm(back_ref[rows, :], qh[...]) + mm(back_ref[rows, :], ql[...])
        out_ref[s, 0] = value[:, :LANES]
        out_ref[s, 1] = value[:, LANES:]


def kerr_call(received, perm, back, chi_lines):
    shards, _, local, _ = received.shape
    modes = shards * local
    groups = HG_ORDER // GROUP
    spread, table, gather, flip = kerr_constants()
    operands = (received, perm, back, spread, table, gather, flip, chi_lines)
    return pl.pallas_call(
        kerr_kernel,
        out_shape=jax.ShapeDtypeStruct((shards, 2, local, LANES), f32),
        in_specs=[pl.BlockSpec(memory_space=pltpu.VMEM)] * len(operands),
        out_specs=pl.BlockSpec(memory_space=pltpu.VMEM),
        scratch_shapes=[
            pltpu.VMEM((modes, 4 * LANES), bf16),
            pltpu.VMEM((modes, 4 * LANES), bf16),
            pltpu.VMEM((groups, 3 * GROUP * HG_ORDER, 4 * LANES), bf16),
            pltpu.VMEM((GRID, 2 * HG_ORDER, 4 * LANES), bf16),
            pltpu.VMEM((groups, 3 * GRID * GROUP, 2 * LANES), bf16),
            pltpu.VMEM((modes, 2 * LANES), bf16),
            pltpu.VMEM((modes, 2 * LANES), bf16),
        ],
        compiler_params=pltpu.CompilerParams(vmem_limit_bytes=48 << 20),
        cost_estimate=pl.CostEstimate(
            flops=30_000_000_000, bytes_accessed=12 << 20, transcendentals=0
        ),
        name="kerr_chunk",
    )(*operands)


def small_fft(values, sign):
    count = len(values)
    if count == 1:
        return values
    evens = small_fft(values[0::2], sign)
    odds = small_fft(values[1::2], sign)
    lower, upper = [], []
    for k in range(count // 2):
        er, ei = evens[k]
        dr, di = odds[k]
        if k == 0:
            tr, ti = dr, di
        elif 4 * k == count:
            tr, ti = (-di, dr) if sign > 0 else (di, -dr)
        else:
            c = math.cos(2 * math.pi * k / count)
            s = sign * math.sin(2 * math.pi * k / count)
            tr, ti = dr * c - di * s, dr * s + di * c
        lower.append((er + tr, ei + ti))
        upper.append((er - tr, ei - ti))
    return lower + upper


def dispersion_constants(length):
    outer = length // LANES
    k = np.arange(outer)[:, None] * np.arange(LANES)[None, :] % length
    twiddle = np.stack([np.cos(2 * np.pi * k / length), np.sin(2 * np.pi * k / length)])
    angle = 2 * np.pi * (np.arange(LANES)[:, None] * np.arange(LANES)[None, :] % LANES) / LANES
    c, s = np.cos(angle), np.sin(angle)
    out = [twiddle.astype(np.float32)]
    for sign in (-1.0, 1.0):
        high, low = host_parts(np.block([[c, sign * s], [-sign * s, c]]))
        out.append(np.concatenate([high, high, low], axis=0))
    return out


def dispersion_kernel(chunks, *refs):
    sources = refs[:chunks]
    cos_ref, sin_ref, tw_ref, fore_ref, back_ref, out_ref, work = refs[chunks:]
    shards = sources[0].shape[0]
    outer, rows, _ = cos_ref.shape
    scale = 1.0 / (outer * LANES)

    def triple(value):
        high, low = parts(value)
        return jnp.concatenate([high, low, high], axis=1)

    for h in range(rows // 8):
        at = slice(h * 8, h * 8 + 8)
        signal = [
            (sources[a // shards][a % shards, 0, at, :], sources[a // shards][a % shards, 1, at, :])
            for a in range(outer)
        ]
        for k, (re, im) in enumerate(small_fft(signal, -1)):
            c, s = tw_ref[0, k : k + 1, :], tw_ref[1, k : k + 1, :]
            work[k, at, 0:LANES] = re * c + im * s
            work[k, at, LANES : 2 * LANES] = im * c - re * s

    block = 8
    for b in range(outer // block):
        ks = slice(b * block, (b + 1) * block)
        value = work[ks].reshape(block * rows, 2 * LANES)
        value = mm(triple(value), fore_ref[...])
        re, im = value[:, :LANES], value[:, LANES:]
        c = cos_ref[ks].reshape(block * rows, LANES)
        s = sin_ref[ks].reshape(block * rows, LANES)
        value = jnp.concatenate([re * c + im * s, im * c - re * s], axis=1)
        value = mm(triple(value), back_ref[...])
        work[ks] = value.reshape(block, rows, 2 * LANES)

    for h in range(rows // 8):
        at = slice(h * 8, h * 8 + 8)
        spectrum = []
        for k in range(outer):
            re, im = work[k, at, 0:LANES], work[k, at, LANES : 2 * LANES]
            c, s = tw_ref[0, k : k + 1, :] * scale, tw_ref[1, k : k + 1, :] * scale
            spectrum.append((re * c - im * s, re * s + im * c))
        for a, (re, im) in enumerate(small_fft(spectrum, 1)):
            out_ref[0, 0, at, a * LANES : (a + 1) * LANES] = re
            out_ref[0, 1, at, a * LANES : (a + 1) * LANES] = im


def dispersion_call(sources, cos, sin):
    shards, _, modes, _ = sources[0].shape
    outer = cos.shape[0]
    length = outer * LANES
    rows = 16
    twiddle, fore, back = dispersion_constants(length)
    whole = lambda a: pl.BlockSpec(a.shape, lambda i: (0,) * a.ndim)
    return pl.pallas_call(
        functools.partial(dispersion_kernel, len(sources)),
        grid=(modes // rows,),
        out_shape=jax.ShapeDtypeStruct((1, 2, modes, length), f32),
        in_specs=[pl.BlockSpec((shards, 2, rows, LANES), lambda i: (0, 0, i, 0))] * len(sources)
        + [pl.BlockSpec((outer, rows, LANES), lambda i: (0, i, 0))] * 2
        + [whole(twiddle), whole(fore), whole(back)],
        out_specs=pl.BlockSpec((1, 2, rows, length), lambda i: (0, 0, i, 0)),
        scratch_shapes=[pltpu.VMEM((outer, rows, 2 * LANES), f32)],
        compiler_params=pltpu.CompilerParams(vmem_limit_bytes=40 << 20),
        cost_estimate=pl.CostEstimate(
            flops=4_000_000_000, bytes_accessed=16 << 20, transcendentals=0
        ),
        name="dispersion",
    )(*sources, cos, sin, twiddle, fore, back)


def on_device(forward, cotangent, mode_order, region, chi, phase, loss):
    shards = lax.axis_size("ma")
    depth = lax.axis_size("gz")
    local, length = forward.shape[2], forward.shape[3]
    modes = mode_order.shape[0]
    width = shards * LANES
    chunks = length // width
    outer = length // LANES

    order = jnp.arange(modes, dtype=jnp.int32)
    perm = (order[:, None] == mode_order[None, :]).astype(bf16)
    back = (mode_order[:, None] == order[None, :]).astype(bf16)
    matches = region.T[:, :, None] == jnp.arange(REGIONS, dtype=jnp.int32)[None, None, :]
    chi_lines = gamma_kerr * jnp.sum(jnp.where(matches, chi[None, None, :], 0.0), axis=-1)

    def chunk(array, c):
        piece = array[0, :, :, c * width : (c + 1) * width]
        return piece.reshape(2, local, shards, LANES).transpose(2, 0, 1, 3)

    cots = [chunk(cotangent, c) for c in range(chunks)]
    received = [
        lax.all_to_all(
            jnp.concatenate([chunk(forward, c), cots[c]], axis=1), "ma", 0, 0, tiled=True
        )
        for c in range(chunks)
    ]
    turned = phase.reshape(local, LANES, outer).transpose(2, 0, 1)
    cos, sin = jnp.cos(turned), jnp.sin(turned)

    to_even = [(i + 1, i) for i in range(0, depth, 2)]
    to_odd = [(i, i + 1) for i in range(0, depth, 2)]
    to_chip = [(i + 2, i) for i in range(0, depth - 2, 2)]
    own = loss[0][None, None, :, None]
    pair = (loss[0] * lax.ppermute(loss[0], "gz", to_even))[None, None, :, None]

    sources = []
    for c in range(chunks):
        kerr = kerr_call(received[c], perm, back, chi_lines)
        source = cots[c] + lax.all_to_all(kerr, "ma", 0, 0, tiled=True)
        both = source + own * lax.ppermute(source, "gz", to_even)
        value, later = both, jnp.zeros_like(both)
        for _ in range(depth // 2 - 1):
            later = lax.ppermute(value, "gz", to_chip)
            value = both + pair * later
        sources.append(value + own * lax.ppermute(later, "gz", to_odd))
    return dispersion_call(sources, cos, sin)


def solution(mesh):
    in_specs = (
        P("gz", None, "ma", None),
        P("gz", None, "ma", None),
        P(),
        P(),
        P(),
        P("ma", None),
        P("gz", "ma"),
    )
    out_specs = P("gz", None, "ma", None)
    return jax.shard_map(
        on_device, mesh=mesh, in_specs=in_specs, out_specs=out_specs, check_vma=False
    )
```

```python
import functools
import math

import jax
import jax.numpy as jnp
import ml_dtypes
import numpy as np
from jax import lax
from jax.experimental import pallas as pl
from jax.experimental.pallas import tpu as pltpu
from jax.sharding import PartitionSpec as P

HG_ORDER = 32
GRID = 128
REGIONS = 8
LANES = 128
GROUP = 8

gamma_kerr = 2.0
half_width = 10.0

f32 = jnp.float32
bf16 = jnp.bfloat16


def hermite_table(grid_points, degrees):
    spacing = 2.0 * half_width / grid_points
    coords = (np.arange(grid_points, dtype=np.float64) - (grid_points - 1) / 2.0) * spacing
    columns = [np.exp(-0.5 * coords * coords) * math.pi ** (-0.25)]
    columns.append(math.sqrt(2.0) * coords * columns[0])
    for degree in range(2, degrees):
        columns.append(
            math.sqrt(2.0 / degree) * coords * columns[degree - 1]
            - math.sqrt((degree - 1.0) / degree) * columns[degree - 2]
        )
    return (np.stack(columns, axis=1) * math.sqrt(spacing)).astype(np.float32)


def host_parts(array):
    array = np.asarray(array, np.float32)
    high = array.astype(ml_dtypes.bfloat16)
    low = (array - high.astype(np.float32)).astype(ml_dtypes.bfloat16)
    return high, low


def parts(value):
    high = value.astype(bf16)
    low = (value - high.astype(f32)).astype(bf16)
    return high, low


def mm(left, right):
    return jnp.dot(left, right, preferred_element_type=f32)


def kerr_constants():
    table = hermite_table(GRID, HG_ORDER)
    eye = np.eye(GROUP, dtype=np.float32)
    spread = np.einsum("yq,ab->yabq", table, eye).reshape(GRID * GROUP, GROUP * HG_ORDER)
    gather = np.einsum("yq,ab->aqyb", table, eye).reshape(GROUP * HG_ORDER, GRID * GROUP)
    spread_high, spread_low = host_parts(spread)
    gather_high, gather_low = host_parts(gather)
    table_high, table_low = host_parts(table)
    return (
        np.concatenate([spread_high, spread_high, spread_low], axis=1),
        np.concatenate([table_high, table_high, table_low], axis=1),
        np.concatenate([gather_high, gather_high, gather_low], axis=1),
        np.ascontiguousarray(table.T),
    )


def kerr_kernel(
    x_ref, perm_ref, back_ref, spread_ref, table_ref, gather_ref, flip_ref, chi_ref, *refs
):
    out_ref, xh, xl, p3, g1, r3, qh, ql = refs[-8:]
    shards, _, local, _ = x_ref.shape
    groups = HG_ORDER // GROUP
    span = GROUP * HG_ORDER

    @pl.loop(0, shards)
    def _(s):
        value = jnp.concatenate([x_ref[s, c] for c in range(4)], axis=1)
        high, low = parts(value)
        rows = pl.ds(pl.multiple_of(s * local, local), local)
        xh[rows, :] = high
        xl[rows, :] = low

    @pl.loop(0, groups)
    def _(g):
        rows = pl.ds(pl.multiple_of(g * span, span), span)
        high = mm(perm_ref[rows, :], xh[...]).astype(bf16)
        p3[g, 0:span, :] = high
        p3[g, 2 * span : 3 * span, :] = high
        p3[g, span : 2 * span, :] = mm(perm_ref[rows, :], xl[...]).astype(bf16)

    points = 16
    for pair in range(groups // 2):

        @pl.loop(0, GRID // points)
        def _(b):
            rows = pl.ds(pl.multiple_of(b * points * GROUP, points * GROUP), points * GROUP)
            ys = pl.ds(b * points, points)
            both = [
                mm(spread_ref[rows, :], p3[2 * pair + i]).reshape(points, GROUP, 4 * LANES)
                for i in range(2)
            ]
            high, low = parts(jnp.concatenate(both, axis=1))
            g1[ys, pair * 16 : pair * 16 + 16, :] = high
            g1[ys, HG_ORDER + pair * 16 : HG_ORDER + pair * 16 + 16, :] = low

    def line(y):
        stored = g1[y]
        grid = mm(table_ref[...], jnp.concatenate([stored, stored[:HG_ORDER]], axis=0))
        er, ei, cr, ci = (grid[:, i * LANES : (i + 1) * LANES] for i in range(4))
        rr, ii = er * er, ei * ei
        intensity = rr + ii
        cross = 2.0 * er * ei
        real = (intensity + 2.0 * rr) * ci - cross * cr
        imag = cross * ci - (intensity + 2.0 * ii) * cr
        high, low = parts(jnp.concatenate([real, imag], axis=1))
        weight_high, weight_low = parts(flip_ref[...] * chi_ref[pl.ds(y, 1), :])
        weights = jnp.concatenate([weight_high, weight_high, weight_low], axis=1)
        return mm(weights, jnp.concatenate([high, low, high], axis=0))

    total = GRID * GROUP
    step_lines = 4

    @pl.loop(0, GRID // step_lines)
    def _(b):
        got = [line(b * step_lines + i) for i in range(step_lines)]
        rows = step_lines * GROUP
        at = pl.multiple_of(b * rows, rows)
        for g in range(groups):
            high, low = parts(
                jnp.concatenate([v[g * GROUP : (g + 1) * GROUP] for v in got], axis=0)
            )
            r3[g, pl.ds(at, rows), :] = high
            r3[g, pl.ds(total + at, rows), :] = low
            r3[g, pl.ds(2 * total + at, rows), :] = high

    @pl.loop(0, groups)
    def _(g):
        high, low = parts(mm(gather_ref[...], r3[g]))
        rows = pl.ds(pl.multiple_of(g * span, span), span)
        qh[rows, :] = high
        ql[rows, :] = low

    @pl.loop(0, shards)
    def _(s):
        rows = pl.ds(pl.multiple_of(s * local, local), local)
        value = mm(back_ref[rows, :], qh[...]) + mm(back_ref[rows, :], ql[...])
        out_ref[s, 0] = x_ref[s, 2] + value[:, :LANES]
        out_ref[s, 1] = x_ref[s, 3] + value[:, LANES:]


def kerr_call(received, perm, back, chi_lines, before=()):
    shards, _, local, _ = received.shape
    modes = shards * local
    groups = HG_ORDER // GROUP
    spread, table, gather, flip = kerr_constants()
    operands = (received, perm, back, spread, table, gather, flip, chi_lines)
    return pl.pallas_call(
        kerr_kernel,
        out_shape=jax.ShapeDtypeStruct((shards, 2, local, LANES), f32),
        in_specs=[pl.BlockSpec(memory_space=pltpu.VMEM)] * len(operands)
        + [pl.BlockSpec(memory_space=pl.ANY)] * len(before),
        out_specs=pl.BlockSpec(memory_space=pltpu.VMEM),
        scratch_shapes=[
            pltpu.VMEM((modes, 4 * LANES), bf16),
            pltpu.VMEM((modes, 4 * LANES), bf16),
            pltpu.VMEM((groups, 3 * GROUP * HG_ORDER, 4 * LANES), bf16),
            pltpu.VMEM((GRID, 2 * HG_ORDER, 4 * LANES), bf16),
            pltpu.VMEM((groups, 3 * GRID * GROUP, 2 * LANES), bf16),
            pltpu.VMEM((modes, 2 * LANES), bf16),
            pltpu.VMEM((modes, 2 * LANES), bf16),
        ],
        compiler_params=pltpu.CompilerParams(vmem_limit_bytes=48 << 20),
        cost_estimate=pl.CostEstimate(
            flops=30_000_000_000, bytes_accessed=12 << 20, transcendentals=0
        ),
        name="kerr_chunk",
    )(*operands, *before)


def pack_kernel(forward_ref, cot_ref, *refs):
    out_ref = refs[-1]
    out_ref[0, 0:2] = forward_ref[0]
    out_ref[0, 2:4] = cot_ref[0]


def pack_call(forward, cotangent, c, shards, before=()):
    local = forward.shape[2]
    piece = pl.BlockSpec((1, 2, local, LANES), lambda i: (0, 0, 0, c * shards + i))
    return pl.pallas_call(
        pack_kernel,
        grid=(shards,),
        out_shape=jax.ShapeDtypeStruct((shards, 4, local, LANES), f32),
        in_specs=[piece, piece] + [pl.BlockSpec(memory_space=pl.ANY)] * len(before),
        out_specs=pl.BlockSpec((1, 4, local, LANES), lambda i: (i, 0, 0, 0)),
        compiler_params=pltpu.CompilerParams(vmem_limit_bytes=16 << 20),
        cost_estimate=pl.CostEstimate(flops=0, bytes_accessed=4 << 20, transcendentals=0),
        name="pack_chunk",
    )(forward, cotangent, *before)


def carry_kernel(factor_ref, *refs):
    out_ref = refs[-1]
    for i in range(len(refs) // 2):
        for c in range(2):
            value, later = refs[2 * i][0, c], refs[2 * i + 1][0, c]
            out_ref[0, 2 * i + c] = value + factor_ref[0] * later


def carry_call(pairs, factor):
    shards, _, local, _ = pairs[0][0].shape
    piece = pl.BlockSpec((1, 2, local, LANES), lambda i: (i, 0, 0, 0))
    flat = [array for pair in pairs for array in pair]
    return pl.pallas_call(
        carry_kernel,
        grid=(shards,),
        out_shape=jax.ShapeDtypeStruct((shards, len(flat), local, LANES), f32),
        in_specs=[pl.BlockSpec((1, local, LANES), lambda i: (i, 0, 0))] + [piece] * len(flat),
        out_specs=pl.BlockSpec((1, len(flat), local, LANES), lambda i: (i, 0, 0, 0)),
        compiler_params=pltpu.CompilerParams(vmem_limit_bytes=16 << 20),
        cost_estimate=pl.CostEstimate(
            flops=0, bytes_accessed=(len(pairs) * 3) << 20, transcendentals=0
        ),
        name="carry",
    )(factor, *flat)


def small_fft(values, sign):
    count = len(values)
    if count == 1:
        return values
    evens = small_fft(values[0::2], sign)
    odds = small_fft(values[1::2], sign)
    lower, upper = [], []
    for k in range(count // 2):
        er, ei = evens[k]
        dr, di = odds[k]
        if k == 0:
            tr, ti = dr, di
        elif 4 * k == count:
            tr, ti = (-di, dr) if sign > 0 else (di, -dr)
        else:
            c = math.cos(2 * math.pi * k / count)
            s = sign * math.sin(2 * math.pi * k / count)
            tr, ti = dr * c - di * s, dr * s + di * c
        lower.append((er + tr, ei + ti))
        upper.append((er - tr, ei - ti))
    return lower + upper


def dispersion_constants(length):
    outer = length // LANES
    k = np.arange(outer)[:, None] * np.arange(LANES)[None, :] % length
    twiddle = np.stack([np.cos(2 * np.pi * k / length), np.sin(2 * np.pi * k / length)])
    angle = 2 * np.pi * (np.arange(LANES)[:, None] * np.arange(LANES)[None, :] % LANES) / LANES
    c, s = np.cos(angle), np.sin(angle)
    out = [twiddle.astype(np.float32)]
    for sign in (-1.0, 1.0):
        high, low = host_parts(np.block([[c, sign * s], [-sign * s, c]]))
        out.append(np.concatenate([high, high, low], axis=0))
    return out


def dispersion_kernel(chunks, *refs):
    sources = refs[:chunks]
    cos_ref, sin_ref, tw_ref, fore_ref, back_ref, out_ref, work = refs[chunks:]
    shards = sources[0].shape[0]
    outer, rows, _ = cos_ref.shape
    scale = 1.0 / (outer * LANES)

    def triple(value):
        high, low = parts(value)
        return jnp.concatenate([high, low, high], axis=1)

    for h in range(rows // 8):
        at = slice(h * 8, h * 8 + 8)
        signal = [
            (ref[d, 2 * c, at, :], ref[d, 2 * c + 1, at, :])
            for ref in sources
            for c in range(ref.shape[1] // 2)
            for d in range(shards)
        ]
        for k, (re, im) in enumerate(small_fft(signal, -1)):
            c, s = tw_ref[0, k : k + 1, :], tw_ref[1, k : k + 1, :]
            work[k, at, 0:LANES] = re * c + im * s
            work[k, at, LANES : 2 * LANES] = im * c - re * s

    block = 8
    for b in range(outer // block):
        ks = slice(b * block, (b + 1) * block)
        value = work[ks].reshape(block * rows, 2 * LANES)
        value = mm(triple(value), fore_ref[...])
        re, im = value[:, :LANES], value[:, LANES:]
        c = cos_ref[ks].reshape(block * rows, LANES)
        s = sin_ref[ks].reshape(block * rows, LANES)
        value = jnp.concatenate([re * c + im * s, im * c - re * s], axis=1)
        value = mm(triple(value), back_ref[...])
        work[ks] = value.reshape(block, rows, 2 * LANES)

    for h in range(rows // 8):
        at = slice(h * 8, h * 8 + 8)
        spectrum = []
        for k in range(outer):
            re, im = work[k, at, 0:LANES], work[k, at, LANES : 2 * LANES]
            c, s = tw_ref[0, k : k + 1, :] * scale, tw_ref[1, k : k + 1, :] * scale
            spectrum.append((re * c - im * s, re * s + im * c))
        for a, (re, im) in enumerate(small_fft(spectrum, 1)):
            out_ref[0, 0, at, a * LANES : (a + 1) * LANES] = re
            out_ref[0, 1, at, a * LANES : (a + 1) * LANES] = im


def dispersion_call(sources, cos, sin):
    modes = sources[0].shape[2]
    outer = cos.shape[0]
    length = outer * LANES
    rows = 16
    twiddle, fore, back = dispersion_constants(length)
    whole = lambda a: pl.BlockSpec(a.shape, lambda i: (0,) * a.ndim)
    return pl.pallas_call(
        functools.partial(dispersion_kernel, len(sources)),
        grid=(modes // rows,),
        out_shape=jax.ShapeDtypeStruct((1, 2, modes, length), f32),
        in_specs=[
            pl.BlockSpec(a.shape[:2] + (rows, LANES), lambda i: (0, 0, i, 0)) for a in sources
        ]
        + [pl.BlockSpec((outer, rows, LANES), lambda i: (0, i, 0))] * 2
        + [whole(twiddle), whole(fore), whole(back)],
        out_specs=pl.BlockSpec((1, 2, rows, length), lambda i: (0, 0, i, 0)),
        scratch_shapes=[pltpu.VMEM((outer, rows, 2 * LANES), f32)],
        compiler_params=pltpu.CompilerParams(vmem_limit_bytes=40 << 20),
        cost_estimate=pl.CostEstimate(
            flops=4_000_000_000, bytes_accessed=16 << 20, transcendentals=0
        ),
        name="dispersion",
    )(*sources, cos, sin, twiddle, fore, back)


def on_device(forward, cotangent, mode_order, region, chi, phase, loss):
    shards = lax.axis_size("ma")
    depth = lax.axis_size("gz")
    local, length = forward.shape[2], forward.shape[3]
    modes = mode_order.shape[0]
    width = shards * LANES
    chunks = length // width
    outer = length // LANES

    order = jnp.arange(modes, dtype=jnp.int32)
    perm = (order[:, None] == mode_order[None, :]).astype(bf16)
    back = (mode_order[:, None] == order[None, :]).astype(bf16)
    matches = region.T[:, :, None] == jnp.arange(REGIONS, dtype=jnp.int32)[None, None, :]
    chi_lines = gamma_kerr * jnp.sum(jnp.where(matches, chi[None, None, :], 0.0), axis=-1)

    turned = phase.reshape(local, LANES, outer).transpose(2, 0, 1)
    cos, sin = jnp.cos(turned), jnp.sin(turned)

    to_even = [(i + 1, i) for i in range(0, depth, 2)]
    to_odd = [(i, i + 1) for i in range(0, depth, 2)]
    to_chip = [(i + 2, i) for i in range(0, depth - 2, 2)]
    kept = lax.all_gather(loss[0], "ma")
    wide = (shards, local, LANES)
    own = jnp.broadcast_to(kept[:, :, None], wide)
    pair = jnp.broadcast_to((kept * lax.ppermute(kept, "gz", to_even))[:, :, None], wide)

    def exchange(array):
        return lax.all_to_all(array, "ma", 0, 0, tiled=True)

    def scan(source):
        both = carry_call([(source, lax.ppermute(source, "gz", to_even))], own)
        value, later = both, jnp.zeros_like(both)
        for _ in range(depth // 2 - 1):
            later = lax.ppermute(value, "gz", to_chip)
            value = carry_call([(both, later)], pair)
        return value, lax.ppermute(later, "gz", to_odd)

    received, sources, scanned, ready = [], [], [], []
    merged = max(chunks - 2, 0)
    for c in range(min(2, chunks)):
        received.append(exchange(pack_call(forward, cotangent, c, shards, received)))
    for c in range(chunks):
        before = [sources[-1]] if c else [cos, sin]
        if merged and c == chunks - 1:
            ready.append(carry_call(scanned[:merged], own))
            before.append(ready[0])
        sources.append(kerr_call(received[c], perm, back, chi_lines, before))
        scanned.append(scan(sources[-1]))
        if c + 2 < chunks:
            before = [received[-1], sources[-1]]
            received.append(exchange(pack_call(forward, cotangent, c + 2, shards, before)))
    ready += [carry_call([one], own) for one in scanned[merged:]]
    return dispersion_call([exchange(array) for array in ready], cos, sin)


def solution(mesh):
    in_specs = (
        P("gz", None, "ma", None),
        P("gz", None, "ma", None),
        P(),
        P(),
        P(),
        P("ma", None),
        P("gz", "ma"),
    )
    out_specs = P("gz", None, "ma", None)
    return jax.shard_map(
        on_device, mesh=mesh, in_specs=in_specs, out_specs=out_specs, check_vma=False
    )
```

```python
import functools
import math

import jax
import jax.numpy as jnp
import ml_dtypes
import numpy as np
from jax import lax
from jax.experimental import pallas as pl
from jax.experimental.pallas import tpu as pltpu
from jax.sharding import PartitionSpec as P

HG_ORDER = 32
GRID = 128
REGIONS = 8
LANES = 128
GROUP = 8

gamma_kerr = 2.0
half_width = 10.0

f32 = jnp.float32
bf16 = jnp.bfloat16


def hermite_table(grid_points, degrees):
    spacing = 2.0 * half_width / grid_points
    coords = (np.arange(grid_points, dtype=np.float64) - (grid_points - 1) / 2.0) * spacing
    columns = [np.exp(-0.5 * coords * coords) * math.pi ** (-0.25)]
    columns.append(math.sqrt(2.0) * coords * columns[0])
    for degree in range(2, degrees):
        columns.append(
            math.sqrt(2.0 / degree) * coords * columns[degree - 1]
            - math.sqrt((degree - 1.0) / degree) * columns[degree - 2]
        )
    return (np.stack(columns, axis=1) * math.sqrt(spacing)).astype(np.float32)


def host_parts(array):
    array = np.asarray(array, np.float32)
    high = array.astype(ml_dtypes.bfloat16)
    low = (array - high.astype(np.float32)).astype(ml_dtypes.bfloat16)
    return high, low


def parts(value):
    high = value.astype(bf16)
    low = (value - high.astype(f32)).astype(bf16)
    return high, low


def mm(left, right):
    return jnp.dot(left, right, preferred_element_type=f32)


def kerr_constants():
    table = hermite_table(GRID, HG_ORDER)
    eye = np.eye(GROUP, dtype=np.float32)
    spread = np.einsum("yq,ab->yabq", table, eye).reshape(GRID * GROUP, GROUP * HG_ORDER)
    gather = np.einsum("yq,ab->aqyb", table, eye).reshape(GROUP * HG_ORDER, GRID * GROUP)
    spread_high, spread_low = host_parts(spread)
    gather_high, gather_low = host_parts(gather)
    table_high, table_low = host_parts(table)
    return (
        np.concatenate([spread_high, spread_high, spread_low], axis=1),
        np.concatenate([table_high, table_high, table_low], axis=1),
        np.concatenate([gather_high, gather_high, gather_low], axis=1),
        np.ascontiguousarray(table.T),
    )


def kerr_kernel(
    x_ref, perm_ref, back_ref, spread_ref, table_ref, gather_ref, flip_ref, chi_ref, *refs
):
    out_ref, xh, xl, p3, g1, r3, qh, ql = refs[-8:]
    shards, _, local, _ = x_ref.shape
    groups = HG_ORDER // GROUP
    span = GROUP * HG_ORDER

    @pl.loop(0, shards)
    def _(s):
        value = jnp.concatenate([x_ref[s, c] for c in range(4)], axis=1)
        high, low = parts(value)
        rows = pl.ds(pl.multiple_of(s * local, local), local)
        xh[rows, :] = high
        xl[rows, :] = low

    @pl.loop(0, groups)
    def _(g):
        rows = pl.ds(pl.multiple_of(g * span, span), span)
        high = mm(perm_ref[rows, :], xh[...]).astype(bf16)
        p3[g, 0:span, :] = high
        p3[g, 2 * span : 3 * span, :] = high
        p3[g, span : 2 * span, :] = mm(perm_ref[rows, :], xl[...]).astype(bf16)

    points = 16
    for pair in range(groups // 2):

        @pl.loop(0, GRID // points)
        def _(b):
            rows = pl.ds(pl.multiple_of(b * points * GROUP, points * GROUP), points * GROUP)
            ys = pl.ds(b * points, points)
            both = [
                mm(spread_ref[rows, :], p3[2 * pair + i]).reshape(points, GROUP, 4 * LANES)
                for i in range(2)
            ]
            high, low = parts(jnp.concatenate(both, axis=1))
            g1[ys, pair * 16 : pair * 16 + 16, :] = high
            g1[ys, HG_ORDER + pair * 16 : HG_ORDER + pair * 16 + 16, :] = low

    def line(y):
        stored = g1[y]
        grid = mm(table_ref[...], jnp.concatenate([stored, stored[:HG_ORDER]], axis=0))
        er, ei, cr, ci = (grid[:, i * LANES : (i + 1) * LANES] for i in range(4))
        rr, ii = er * er, ei * ei
        intensity = rr + ii
        cross = 2.0 * er * ei
        real = (intensity + 2.0 * rr) * ci - cross * cr
        imag = cross * ci - (intensity + 2.0 * ii) * cr
        high, low = parts(jnp.concatenate([real, imag], axis=1))
        weight_high, weight_low = parts(flip_ref[...] * chi_ref[pl.ds(y, 1), :])
        weights = jnp.concatenate([weight_high, weight_high, weight_low], axis=1)
        return mm(weights, jnp.concatenate([high, low, high], axis=0))

    total = GRID * GROUP
    step_lines = 4

    @pl.loop(0, GRID // step_lines)
    def _(b):
        got = [line(b * step_lines + i) for i in range(step_lines)]
        rows = step_lines * GROUP
        at = pl.multiple_of(b * rows, rows)
        for g in range(groups):
            high, low = parts(
                jnp.concatenate([v[g * GROUP : (g + 1) * GROUP] for v in got], axis=0)
            )
            r3[g, pl.ds(at, rows), :] = high
            r3[g, pl.ds(total + at, rows), :] = low
            r3[g, pl.ds(2 * total + at, rows), :] = high

    @pl.loop(0, groups)
    def _(g):
        high, low = parts(mm(gather_ref[...], r3[g]))
        rows = pl.ds(pl.multiple_of(g * span, span), span)
        qh[rows, :] = high
        ql[rows, :] = low

    @pl.loop(0, shards)
    def _(s):
        rows = pl.ds(pl.multiple_of(s * local, local), local)
        value = mm(back_ref[rows, :], qh[...]) + mm(back_ref[rows, :], ql[...])
        out_ref[s, 0] = x_ref[s, 2] + value[:, :LANES]
        out_ref[s, 1] = x_ref[s, 3] + value[:, LANES:]


def kerr_call(received, perm, back, chi_lines, before=()):
    shards, _, local, _ = received.shape
    modes = shards * local
    groups = HG_ORDER // GROUP
    spread, table, gather, flip = kerr_constants()
    operands = (received, perm, back, spread, table, gather, flip, chi_lines)
    return pl.pallas_call(
        kerr_kernel,
        out_shape=jax.ShapeDtypeStruct((shards, 2, local, LANES), f32),
        in_specs=[pl.BlockSpec(memory_space=pltpu.VMEM)] * len(operands)
        + [pl.BlockSpec(memory_space=pl.ANY)] * len(before),
        out_specs=pl.BlockSpec(memory_space=pltpu.VMEM),
        scratch_shapes=[
            pltpu.VMEM((modes, 4 * LANES), bf16),
            pltpu.VMEM((modes, 4 * LANES), bf16),
            pltpu.VMEM((groups, 3 * GROUP * HG_ORDER, 4 * LANES), bf16),
            pltpu.VMEM((GRID, 2 * HG_ORDER, 4 * LANES), bf16),
            pltpu.VMEM((groups, 3 * GRID * GROUP, 2 * LANES), bf16),
            pltpu.VMEM((modes, 2 * LANES), bf16),
            pltpu.VMEM((modes, 2 * LANES), bf16),
        ],
        compiler_params=pltpu.CompilerParams(vmem_limit_bytes=48 << 20),
        cost_estimate=pl.CostEstimate(
            flops=56_000_000_000, bytes_accessed=12 << 20, transcendentals=0
        ),
        name="kerr_chunk",
    )(*operands, *before)


def pack_kernel(forward_ref, cot_ref, *refs):
    out_ref = refs[-1]
    out_ref[0, 0:2] = forward_ref[0]
    out_ref[0, 2:4] = cot_ref[0]


def pack_call(forward, cotangent, c, shards, before=()):
    local = forward.shape[2]
    piece = pl.BlockSpec((1, 2, local, LANES), lambda i: (0, 0, 0, c * shards + i))
    return pl.pallas_call(
        pack_kernel,
        grid=(shards,),
        out_shape=jax.ShapeDtypeStruct((shards, 4, local, LANES), f32),
        in_specs=[piece, piece] + [pl.BlockSpec(memory_space=pl.ANY)] * len(before),
        out_specs=pl.BlockSpec((1, 4, local, LANES), lambda i: (i, 0, 0, 0)),
        compiler_params=pltpu.CompilerParams(vmem_limit_bytes=16 << 20),
        cost_estimate=pl.CostEstimate(flops=0, bytes_accessed=4 << 20, transcendentals=0),
        name="pack_chunk",
    )(forward, cotangent, *before)


def carry_kernel(factor_ref, *refs):
    out_ref = refs[-1]
    for i in range(len(refs) // 2):
        for c in range(2):
            value, later = refs[2 * i][0, c], refs[2 * i + 1][0, c]
            out_ref[0, 2 * i + c] = value + factor_ref[0] * later


def carry_call(pairs, factor):
    shards, _, local, _ = pairs[0][0].shape
    piece = pl.BlockSpec((1, 2, local, LANES), lambda i: (i, 0, 0, 0))
    flat = [array for pair in pairs for array in pair]
    return pl.pallas_call(
        carry_kernel,
        grid=(shards,),
        out_shape=jax.ShapeDtypeStruct((shards, len(flat), local, LANES), f32),
        in_specs=[pl.BlockSpec((1, local, LANES), lambda i: (i, 0, 0))] + [piece] * len(flat),
        out_specs=pl.BlockSpec((1, len(flat), local, LANES), lambda i: (i, 0, 0, 0)),
        compiler_params=pltpu.CompilerParams(vmem_limit_bytes=16 << 20),
        cost_estimate=pl.CostEstimate(
            flops=0, bytes_accessed=(len(pairs) * 3) << 20, transcendentals=0
        ),
        name="carry",
    )(factor, *flat)


def small_fft(values, sign):
    count = len(values)
    if count == 1:
        return values
    evens = small_fft(values[0::2], sign)
    odds = small_fft(values[1::2], sign)
    lower, upper = [], []
    for k in range(count // 2):
        er, ei = evens[k]
        dr, di = odds[k]
        if k == 0:
            tr, ti = dr, di
        elif 4 * k == count:
            tr, ti = (-di, dr) if sign > 0 else (di, -dr)
        else:
            c = math.cos(2 * math.pi * k / count)
            s = sign * math.sin(2 * math.pi * k / count)
            tr, ti = dr * c - di * s, dr * s + di * c
        lower.append((er + tr, ei + ti))
        upper.append((er - tr, ei - ti))
    return lower + upper


def dispersion_constants(length):
    outer = length // LANES
    k = np.arange(outer)[:, None] * np.arange(LANES)[None, :] % length
    twiddle = np.stack([np.cos(2 * np.pi * k / length), np.sin(2 * np.pi * k / length)])
    angle = 2 * np.pi * (np.arange(LANES)[:, None] * np.arange(LANES)[None, :] % LANES) / LANES
    c, s = np.cos(angle), np.sin(angle)
    out = [twiddle.astype(np.float32)]
    for sign in (-1.0, 1.0):
        high, low = host_parts(np.block([[c, sign * s], [-sign * s, c]]))
        out.append(np.concatenate([high, high, low], axis=0))
    return out


def dispersion_kernel(chunks, *refs):
    sources = refs[:chunks]
    cos_ref, sin_ref, tw_ref, fore_ref, back_ref, out_ref, work = refs[chunks:]
    shards = sources[0].shape[0]
    outer, rows, _ = cos_ref.shape
    scale = 1.0 / (outer * LANES)

    def triple(value):
        high, low = parts(value)
        return jnp.concatenate([high, low, high], axis=1)

    for h in range(rows // 8):
        at = slice(h * 8, h * 8 + 8)
        signal = [
            (ref[d, 2 * c, at, :], ref[d, 2 * c + 1, at, :])
            for ref in sources
            for c in range(ref.shape[1] // 2)
            for d in range(shards)
        ]
        for k, (re, im) in enumerate(small_fft(signal, -1)):
            c, s = tw_ref[0, k : k + 1, :], tw_ref[1, k : k + 1, :]
            work[k, at, 0:LANES] = re * c + im * s
            work[k, at, LANES : 2 * LANES] = im * c - re * s

    block = 8
    for b in range(outer // block):
        ks = slice(b * block, (b + 1) * block)
        value = work[ks].reshape(block * rows, 2 * LANES)
        value = mm(triple(value), fore_ref[...])
        re, im = value[:, :LANES], value[:, LANES:]
        c = cos_ref[ks].reshape(block * rows, LANES)
        s = sin_ref[ks].reshape(block * rows, LANES)
        value = jnp.concatenate([re * c + im * s, im * c - re * s], axis=1)
        value = mm(triple(value), back_ref[...])
        work[ks] = value.reshape(block, rows, 2 * LANES)

    for h in range(rows // 8):
        at = slice(h * 8, h * 8 + 8)
        spectrum = []
        for k in range(outer):
            re, im = work[k, at, 0:LANES], work[k, at, LANES : 2 * LANES]
            c, s = tw_ref[0, k : k + 1, :] * scale, tw_ref[1, k : k + 1, :] * scale
            spectrum.append((re * c - im * s, re * s + im * c))
        for a, (re, im) in enumerate(small_fft(spectrum, 1)):
            out_ref[0, 0, at, a * LANES : (a + 1) * LANES] = re
            out_ref[0, 1, at, a * LANES : (a + 1) * LANES] = im


def dispersion_call(sources, cos, sin):
    modes = sources[0].shape[2]
    outer = cos.shape[0]
    length = outer * LANES
    rows = 16
    twiddle, fore, back = dispersion_constants(length)
    whole = lambda a: pl.BlockSpec(a.shape, lambda i: (0,) * a.ndim)
    return pl.pallas_call(
        functools.partial(dispersion_kernel, len(sources)),
        grid=(modes // rows,),
        out_shape=jax.ShapeDtypeStruct((1, 2, modes, length), f32),
        in_specs=[
            pl.BlockSpec(a.shape[:2] + (rows, LANES), lambda i: (0, 0, i, 0)) for a in sources
        ]
        + [pl.BlockSpec((outer, rows, LANES), lambda i: (0, i, 0))] * 2
        + [whole(twiddle), whole(fore), whole(back)],
        out_specs=pl.BlockSpec((1, 2, rows, length), lambda i: (0, 0, i, 0)),
        scratch_shapes=[pltpu.VMEM((outer, rows, 2 * LANES), f32)],
        compiler_params=pltpu.CompilerParams(vmem_limit_bytes=40 << 20),
        cost_estimate=pl.CostEstimate(
            flops=4_000_000_000, bytes_accessed=16 << 20, transcendentals=0
        ),
        name="dispersion",
    )(*sources, cos, sin, twiddle, fore, back)


def on_device(forward, cotangent, mode_order, region, chi, phase, loss):
    shards = lax.axis_size("ma")
    depth = lax.axis_size("gz")
    local, length = forward.shape[2], forward.shape[3]
    modes = mode_order.shape[0]
    width = shards * LANES
    chunks = length // width
    outer = length // LANES

    order = jnp.arange(modes, dtype=jnp.int32)
    perm = (order[:, None] == mode_order[None, :]).astype(bf16)
    back = (mode_order[:, None] == order[None, :]).astype(bf16)
    matches = region.T[:, :, None] == jnp.arange(REGIONS, dtype=jnp.int32)[None, None, :]
    chi_lines = gamma_kerr * jnp.sum(jnp.where(matches, chi[None, None, :], 0.0), axis=-1)

    turned = phase.reshape(local, LANES, outer).transpose(2, 0, 1)
    cos, sin = jnp.cos(turned), jnp.sin(turned)

    to_even = [(i + 1, i) for i in range(0, depth, 2)]
    to_odd = [(i, i + 1) for i in range(0, depth, 2)]
    to_chip = [(i + 2, i) for i in range(0, depth - 2, 2)]
    kept = lax.all_gather(loss[0], "ma")
    wide = (shards, local, LANES)
    own = jnp.broadcast_to(kept[:, :, None], wide)
    pair = jnp.broadcast_to((kept * lax.ppermute(kept, "gz", to_even))[:, :, None], wide)

    def exchange(array):
        return lax.all_to_all(array, "ma", 0, 0, tiled=True)

    def scan(source):
        both = carry_call([(source, lax.ppermute(source, "gz", to_even))], own)
        value, later = both, jnp.zeros_like(both)
        for _ in range(depth // 2 - 1):
            later = lax.ppermute(value, "gz", to_chip)
            value = carry_call([(both, later)], pair)
        return value, lax.ppermute(later, "gz", to_odd)

    received, sources, scanned, ready = [], [], [], []
    merged = max(chunks - 2, 0)
    for c in range(min(2, chunks)):
        before = received + [cos, sin, perm, back, chi_lines, own, pair] * c
        received.append(exchange(pack_call(forward, cotangent, c, shards, before)))
    for c in range(chunks):
        before = [sources[-1]] if c else [cos, sin]
        if merged and c == chunks - 1:
            ready.append(carry_call(scanned[:merged], own))
            before.append(ready[0])
        sources.append(kerr_call(received[c], perm, back, chi_lines, before))
        scanned.append(scan(sources[-1]))
        if c + 2 < chunks:
            before = [received[-1], sources[-1]]
            received.append(exchange(pack_call(forward, cotangent, c + 2, shards, before)))
    ready += [carry_call([one], own) for one in scanned[merged:]]
    return dispersion_call([exchange(array) for array in ready], cos, sin)


def solution(mesh):
    in_specs = (
        P("gz", None, "ma", None),
        P("gz", None, "ma", None),
        P(),
        P(),
        P(),
        P("ma", None),
        P("gz", "ma"),
    )
    out_specs = P("gz", None, "ma", None)
    return jax.shard_map(
        on_device, mesh=mesh, in_specs=in_specs, out_specs=out_specs, check_vma=False
    )
```
